32 devices in a mesh: cls: 4 (over z), ptl: 8 (over y, x, core).
Axes of the slice: x: 2, y: 2, z: 4, core: 2. Of those that a mesh axis runs over, the one named last changes fastest.
Arguments:
- particles: bfloat16 [16384, 64, 128], P(('cls', 'ptl')), may hold values from -6 to 6
- references: bfloat16 [64, 200, 128], P('ptl', 'cls'), may hold values from -0.029907227 to 0.029907227
- best_class: int32 [16384], P(('cls', 'ptl')), may hold values from 0 to 199, as said below
- best_turn: int32 [16384], P(('cls', 'ptl')), may hold values from 0 to 35
Outputs:
- best_score: float32 [16384], P(('cls', 'ptl'))
- new_references: float32 [64, 200, 128], P('ptl', 'cls')
The draws below stay inside these ranges and needn't reach their ends.
Inputs may be any that keep to these rules, and one draw needn't show every extreme that they name: `best_class`: in each aligned block of 512 rows (the particles of one device), at most 160 classes lie in one class shard, classes k * 50 to (k + 1) * 50 - 1; some class shard receives exactly 160 from every block.
All inputs are finite; a program needn't handle non-finite values.
Results may differ from the reference program's by a relative error of at most 0.0048.
Values may be sent and summed in bfloat16 or wider, within the bound.
A program may use at most 192 MiB of HBM per device.

```python
import math
import jax
import jax.numpy as jnp
from jax import lax

RHO = 64
NA = 128
ROTS = 36
C_DEV = 50
P_DEV = 512
SLOT_CAP = 160
CLASSES = 200
PARTICLES = 16384


def draw_best_class(key, part):
    owner_count = CLASSES // C_DEV
    block_count = PARTICLES // P_DEV
    slot_count = owner_count * SLOT_CAP
    key_heat, key_full, key_score, key_shuffle, key_first, key_second = jax.random.split(key, 6)
    heat_level = jax.random.randint(key_heat, (owner_count,), 1, 6)
    full_owner = jax.random.randint(key_full, (), 0, owner_count)
    slot_owner = jnp.arange(slot_count, dtype=jnp.int32) // SLOT_CAP
    raw_score = jax.random.randint(key_score, (block_count, slot_count), 0, 4096)
    weighted = raw_score * (6 - heat_level[slot_owner])[None, :]
    weighted = jnp.where((slot_owner == full_owner)[None, :], -1, weighted)
    keyed = weighted * slot_count + jnp.arange(slot_count, dtype=jnp.int32)[None, :]
    chosen = jnp.argsort(keyed, axis=1)[:, :P_DEV]
    shuffle_key = jax.random.randint(key_shuffle, (block_count, P_DEV), 0, 1 << 20) * P_DEV + jnp.arange(P_DEV, dtype=jnp.int32)[None, :]
    shuffle_order = jnp.argsort(shuffle_key, axis=1)
    chosen = jnp.take_along_axis(chosen, shuffle_order, axis=1)
    owner_of = chosen // SLOT_CAP
    first_pick = jax.random.randint(key_first, (block_count, P_DEV), 0, C_DEV)
    second_pick = jax.random.randint(key_second, (block_count, P_DEV), 0, C_DEV)
    local_class = jnp.minimum(first_pick, second_pick)
    return (owner_of * C_DEV + local_class).reshape(PARTICLES).astype(jnp.int32)


def plant(array, rng, smallest, high):
    dims = array.shape
    index_at = [jax.random.randint(jax.random.fold_in(rng, axis), (), 0, dims[axis]) for axis in range(len(dims))]
    array = array.at[tuple(index_at)].set(smallest)
    longest = dims.index(max(dims))
    index_at[longest] = (index_at[longest] + 1) % dims[longest]
    return array.at[tuple(index_at)].set(high)


def levels(stream_key, shape, cuts, smallest, high):
    level, own = 1.0, jax.random.fold_in(stream_key, 6)
    for dim, shards_of in cuts:
        steps = jnp.exp(jax.random.uniform(jax.random.fold_in(own, dim), (shards_of,), jnp.float32, smallest / len(cuts), high / len(cuts)))
        level = level * jnp.repeat(steps, shape[dim] // shards_of).reshape([-1 if axis == dim else 1 for axis in range(len(shape))])
    return level


def scatter_about(rng, shape, scale, bound, cuts=(), held_as=jnp.bfloat16):
    entries = jax.random.normal(rng, shape, jnp.float32) * scale
    if len(cuts) > 0:
        entries = levels(rng, shape, cuts, -0.22, 0.18) * entries
    return jnp.clip(entries, min=-bound, max=bound).astype(held_as)


def setup_inputs(seed: int = 0) -> dict:
    streams_of = jax.random.split(jax.random.key(seed), 5)
    particles = scatter_about(streams_of[0], (PARTICLES, RHO, NA), 1.0, 6.0, ((0, 32),))
    references = scatter_about(streams_of[1], (NA // 2, CLASSES, 2 * RHO), 0.005, 0.029907227, ((0, 8), (1, 4)))
    best_class = draw_best_class(jax.random.fold_in(streams_of[4], 71), 0)
    best_turn = plant(jax.random.randint(streams_of[3], (PARTICLES,), 0, ROTS), jax.random.fold_in(streams_of[3], 1), 0, ROTS - 1).astype(jnp.int32)
    return {"particles": particles, "references": references, "best_class": best_class, "best_turn": best_turn}


def spectrum_table(angles, freq_count):
    position = jnp.arange(angles, dtype=jnp.int32)
    freq_index = jnp.arange(freq_count, dtype=jnp.int32)
    phases = 2.0 * math.pi / angles * (position[:, None] * freq_index[None, :] % angles).astype(jnp.float32)
    factor = 1.0 / math.sqrt(angles)
    return (jnp.concatenate([jnp.cos(phases), -jnp.sin(phases)], axis=1) * factor).astype(jnp.bfloat16)

def rotation_table(freq_count, turns):
    freq_index = jnp.arange(freq_count, dtype=jnp.int32)
    turn_index = jnp.arange(turns, dtype=jnp.int32)
    phases = 2.0 * math.pi / turns * (freq_index[:, None] * turn_index[None, :] % turns).astype(jnp.float32)
    weight = jnp.where(freq_index == 0, 1.0, 2.0).astype(jnp.float32)[:, None]
    return jnp.stack([weight * jnp.cos(phases), -weight * jnp.sin(phases)]).astype(jnp.bfloat16)

def quarter(panel):
    half_width = panel.shape[-1] // 2
    return jnp.concatenate([panel[..., half_width:], -panel[..., :half_width]], axis=-1)

def rotate_back(spectra, turn_of, turns):
    freq_count = spectra.shape[0]
    half_width = spectra.shape[-1] // 2
    freq_index = jnp.arange(freq_count, dtype=jnp.int32)
    phases = 2.0 * math.pi / turns * (freq_index[:, None] * turn_of[None, :] % turns).astype(jnp.float32)
    cosine = jnp.cos(phases)[:, :, None]
    sine_part = jnp.sin(phases)[:, :, None]
    real_part = spectra[..., :half_width].astype(jnp.float32)
    imag_part = spectra[..., half_width:].astype(jnp.float32)
    return jnp.concatenate([real_part * cosine + imag_part * sine_part, imag_part * cosine - real_part * sine_part], axis=-1).astype(jnp.bfloat16)

def reference(particles, references, best_class, best_turn):
    freq_count = NA // 2
    dft_table = spectrum_table(NA, freq_count).astype(jnp.float32)
    turn_table = rotation_table(freq_count, ROTS).astype(jnp.float32)
    panels = references.astype(jnp.float32)
    stacked = jnp.concatenate([panels, quarter(panels)], axis=1)
    class_count = panels.shape[1]
    block_count = PARTICLES // P_DEV
    particle_blocks = particles.reshape(block_count, P_DEV, RHO, NA)
    label_blocks = best_class.reshape(block_count, P_DEV)
    turn_blocks = best_turn.reshape(block_count, P_DEV)
    class_ids = jnp.arange(class_count, dtype=jnp.int32)

    def advance(carried, block_item):
        totals, counts = carried
        particle_block, block_labels, block_turns = block_item
        raw_terms = jnp.einsum('ipa,ak->kip', particle_block.astype(jnp.float32), dft_table)
        spectra = raw_terms.astype(jnp.bfloat16).reshape(2, freq_count, P_DEV, RHO)
        spectra = jnp.transpose(spectra, (1, 2, 0, 3)).reshape(freq_count, P_DEV, 2 * RHO)
        spectra_wide = lax.optimization_barrier(spectra).astype(jnp.float32)
        cross_terms = jnp.einsum('mik,mck->mic', spectra_wide, stacked).astype(jnp.bfloat16)
        cross_terms = lax.optimization_barrier(cross_terms).astype(jnp.float32)
        cross_terms = cross_terms.reshape(freq_count, P_DEV, 2, class_count)
        scores = jnp.einsum('mijc,jmr->irc', cross_terms, turn_table)
        best_block = lax.optimization_barrier(jnp.max(scores, axis=(1, 2)))
        aligned = lax.optimization_barrier(rotate_back(spectra, block_turns, ROTS)).astype(jnp.float32)
        member = (block_labels[None, :] == class_ids[:, None]).astype(jnp.float32)
        totals = totals + jnp.einsum('ci,mik->mck', member, aligned)
        counts = counts + lax.optimization_barrier(jnp.sum(member, axis=1))
        return ((totals, counts), best_block)
    start_totals = jnp.zeros((freq_count, class_count, 2 * RHO), jnp.float32)
    start_counts = jnp.zeros((class_count,), jnp.float32)
    (totals, counts), best_blocks = lax.scan(advance, (start_totals, start_counts), (particle_blocks, label_blocks, turn_blocks))
    new_references = totals / (counts + 1.0)[None, :, None]
    return (best_blocks.reshape(PARTICLES), new_references)
```

```python
import functools
import math

import jax
import jax.numpy as jnp
import numpy as np
from jax import lax
from jax.experimental import pallas as pl
from jax.experimental.pallas import tpu as pltpu
from jax.sharding import PartitionSpec as P

ROTS = 36
LANES = 128
VMEM_LIMIT = 60 * 1024 * 1024
NT = (((1,), (1,)), ((), ()))


def fold_groups(freq_count, turns):
    groups = [[] for _ in range(turns // 2 + 1)]
    for m in range(freq_count):
        rest = m % turns
        if rest <= turns // 2:
            groups[rest].append((m, 1))
        else:
            groups[turns - rest].append((m, -1))
    return groups


def spectrum_table(angles, freq_count):
    position = jnp.arange(angles, dtype=jnp.int32)
    freq_index = jnp.arange(freq_count, dtype=jnp.int32)
    phases = (
        2.0
        * math.pi
        / angles
        * (position[:, None] * freq_index[None, :] % angles).astype(jnp.float32)
    )
    factor = 1.0 / math.sqrt(angles)
    return (jnp.concatenate([jnp.cos(phases), -jnp.sin(phases)], axis=1) * factor).astype(
        jnp.bfloat16
    )


def swap_halves(panel):
    half = panel.shape[-1] // 2
    return pltpu.roll(panel, half, panel.ndim - 1)


def spectra_kernel(
    groups,
    columns,
    step_pairs,
    class_count,
    table_ref,
    low_ref,
    high_ref,
    class_ref,
    cos_ref,
    sin_ref,
    spectra_out,
    sums_ref,
    raw_ref,
    held_ref,
    sem,
):
    step = pl.program_id(0)
    steps = pl.num_programs(0)
    freq_count = len(columns)
    half = LANES // 2
    table = table_ref[...]
    for pair in range(step_pairs):
        rows = jnp.concatenate([low_ref[pair], high_ref[pair]], axis=0)
        raw_ref[pl.ds(pair, 2 * freq_count, stride=step_pairs), :] = lax.dot_general(
            table, rows, NT, preferred_element_type=jnp.float32
        )
    first_half = lax.broadcasted_iota(jnp.int32, (step_pairs, LANES), 1) < half
    own_rows = pl.ds(pl.multiple_of(step * step_pairs, step_pairs), step_pairs)
    for m in range(freq_count):
        real = raw_ref[m * step_pairs : (m + 1) * step_pairs, :]
        imag = raw_ref[(freq_count + m) * step_pairs : (freq_count + m + 1) * step_pairs, :]
        at = slice(columns[m] * LANES, (columns[m] + 1) * LANES)
        held_ref[0, own_rows, at] = jnp.where(first_half, real, swap_halves(imag)).astype(
            jnp.bfloat16
        )
        held_ref[1, own_rows, at] = jnp.where(first_half, swap_halves(real), imag).astype(
            jnp.bfloat16
        )

    def write_back(at):
        rows = pl.ds(pl.multiple_of(at * step_pairs, step_pairs), step_pairs)
        return pltpu.make_async_copy(
            held_ref.at[:, rows, :], spectra_out.at[:, rows, :], sem.at[at]
        )

    write_back(step).start()

    @pl.when(step == steps - 1)
    def _():
        count_p = class_ref.shape[1]
        member = lax.broadcasted_iota(jnp.int32, (class_count, count_p), 0) == class_ref[...]
        lane = lax.broadcasted_iota(jnp.int32, (class_count, LANES), 1)
        flip = jnp.where(lane < half, 1.0, -1.0)
        column = 0
        for folded, group in enumerate(groups):
            width = len(group) * LANES
            at = slice(column, column + width)
            column += width
            weights = jnp.concatenate(
                [
                    jnp.where(member, cos_ref[folded : folded + 1, :], 0.0),
                    jnp.where(member, sin_ref[folded : folded + 1, :], 0.0),
                ],
                axis=0,
            ).astype(jnp.bfloat16)
            half_p = count_p // 2
            both = jnp.dot(
                weights[:, :half_p], held_ref[0, :, at], preferred_element_type=jnp.float32
            ) + jnp.dot(
                weights[:, half_p:], held_ref[1, :, at], preferred_element_type=jnp.float32
            )
            for place, (m, sign) in enumerate(group):
                part = both[:, place * LANES : (place + 1) * LANES]
                turned = swap_halves(part[class_count:]) * flip
                total = part[:class_count] + (turned if sign > 0 else -turned)
                sums_ref[m] = total.astype(jnp.bfloat16)
        for at in range(steps):
            write_back(at).wait()


def score_kernel(
    groups, cos_ref, sin_ref, panels_ref, spectra_ref, best_ref, stacked_ref, even_ref, odd_ref
):
    half = LANES // 2
    class_rows = panels_ref.shape[0]
    tiles = class_rows // 8
    last = len(groups) - 1

    @pl.when(pl.program_id(0) == 0)
    def _():
        lane = lax.broadcasted_iota(jnp.int32, (class_rows, LANES), 1)
        flip = jnp.where(lane < half, 1.0, -1.0)
        column = 0
        for group in groups:
            for m, sign in group:
                weight = 1.0 if m == 0 else 2.0
                panel = panels_ref[:, m * LANES : (m + 1) * LANES].astype(jnp.float32) * weight
                at = slice(column, column + LANES)
                column += LANES
                stacked_ref[0, :, at] = panel.astype(jnp.bfloat16)
                stacked_ref[1, :, at] = (swap_halves(panel) * (flip * sign)).astype(jnp.bfloat16)

    column = 0
    for folded, group in enumerate(groups):
        at = slice(column, column + len(group) * LANES)
        column += len(group) * LANES
        rows = spectra_ref[:, at]
        even = lax.dot_general(
            stacked_ref[0, :, at], rows, NT, preferred_element_type=jnp.float32
        )
        even_ref[:, folded * 8 : (folded + 1) * 8, :] = even.reshape(tiles, 8, -1)
        if 0 < folded < last:
            odd = lax.dot_general(
                stacked_ref[1, :, at], rows, NT, preferred_element_type=jnp.float32
            )
            odd_ref[:, (folded - 1) * 8 : folded * 8, :] = odd.reshape(tiles, 8, -1)

    width = spectra_ref.shape[0]
    cos_mat, sin_mat = cos_ref[...], sin_ref[...]

    def tile_step(tile, best):
        even = jnp.dot(
            cos_mat, even_ref[tile].astype(jnp.bfloat16), preferred_element_type=jnp.float32
        )
        odd = jnp.dot(
            sin_mat, odd_ref[tile].astype(jnp.bfloat16), preferred_element_type=jnp.float32
        )
        best = jnp.maximum(best, jnp.maximum(even[:8], even[last * 8 :]))
        for turn in range(1, last):
            best = jnp.maximum(
                best,
                even[turn * 8 : (turn + 1) * 8] + jnp.abs(odd[(turn - 1) * 8 : turn * 8]),
            )
        return best

    best = lax.fori_loop(0, tiles, tile_step, jnp.full((8, width), -jnp.inf, jnp.float32))
    best_ref[...] = jnp.max(best, axis=0, keepdims=True)


def local(particles, references, best_class, best_turn):
    count_p, cycle_count, angles = particles.shape
    freq_count = angles // 2
    groups = fold_groups(freq_count, ROTS)
    last = len(groups) - 1
    columns = [0] * freq_count
    place = 0
    for group in groups:
        for m, _ in group:
            columns[m] = place
            place += 1
    owners = lax.axis_size("cls")
    freqs_dev, classes_dev, _ = references.shape
    class_count = classes_dev * owners

    own = jnp.transpose(references, (1, 0, 2)).reshape(classes_dev, freqs_dev * LANES)
    panels = lax.all_gather(own, "cls", axis=0, tiled=True)
    panels = lax.all_gather(panels, "ptl", axis=1, tiled=True)
    all_labels = lax.all_gather(best_class, ("cls", "ptl"), axis=0, tiled=True)

    step_pairs = 32
    pairs = count_p // 2
    steps = pairs // step_pairs
    folded_index = jnp.arange(last + 1, dtype=jnp.int32)
    phases = (
        2.0
        * math.pi
        / ROTS
        * (folded_index[:, None] * best_turn[None, :] % ROTS).astype(jnp.float32)
    )
    table = spectrum_table(angles, freq_count).T
    whole = lambda *_: (0, 0)
    spectra, sums = pl.pallas_call(
        functools.partial(spectra_kernel, groups, columns, step_pairs, class_count),
        grid=(steps,),
        out_shape=(
            jax.ShapeDtypeStruct((2, pairs, freq_count * LANES), jnp.bfloat16),
            jax.ShapeDtypeStruct((freq_count, class_count, LANES), jnp.bfloat16),
        ),
        in_specs=[
            pl.BlockSpec((angles, 2 * freq_count), whole),
            pl.BlockSpec((step_pairs, cycle_count, angles), lambda g: (g, 0, 0)),
            pl.BlockSpec((step_pairs, cycle_count, angles), lambda g: (g + steps, 0, 0)),
            pl.BlockSpec((1, count_p), whole),
            pl.BlockSpec((last + 1, count_p), whole),
            pl.BlockSpec((last + 1, count_p), whole),
        ],
        out_specs=(
            pl.BlockSpec(memory_space=pl.ANY),
            pl.BlockSpec((freq_count, class_count, LANES), lambda g: (0, 0, 0)),
        ),
        scratch_shapes=[
            pltpu.VMEM((2 * freq_count * step_pairs, LANES), jnp.float32),
            pltpu.VMEM((2, pairs, freq_count * LANES), jnp.bfloat16),
            pltpu.SemaphoreType.DMA((steps,)),
        ],
        compiler_params=pltpu.CompilerParams(vmem_limit_bytes=VMEM_LIMIT),
        cost_estimate=pl.CostEstimate(
            flops=20_000_000_000, bytes_accessed=20_000_000, transcendentals=0
        ),
        name="spectra",
    )(
        table,
        particles,
        particles,
        best_class.reshape(1, count_p),
        jnp.cos(phases),
        jnp.sin(phases),
    )

    totals = lax.psum_scatter(sums, "ptl", scatter_dimension=0, tiled=True)
    totals = lax.psum_scatter(
        totals.reshape(freqs_dev, owners, classes_dev, LANES), "cls", scatter_dimension=1
    )

    turn_index = np.arange(last + 1)
    turn_phase = 2.0 * math.pi / ROTS * (turn_index[:, None] * turn_index[None, :] % ROTS)
    spread = np.eye(8, dtype=np.float32)
    cos_mat = jnp.asarray(np.kron(np.cos(turn_phase).astype(np.float32), spread), jnp.bfloat16)
    sin_mat = jnp.asarray(
        np.kron(-np.sin(turn_phase[1:last, 1:last]).astype(np.float32), spread), jnp.bfloat16
    )
    spectra = spectra.reshape(count_p, freq_count * LANES)
    block = 256
    best_score = pl.pallas_call(
        functools.partial(score_kernel, groups),
        grid=(count_p // block,),
        out_shape=jax.ShapeDtypeStruct((1, count_p), jnp.float32),
        in_specs=[
            pl.BlockSpec(cos_mat.shape, whole),
            pl.BlockSpec(sin_mat.shape, whole),
            pl.BlockSpec(panels.shape, whole, pipeline_mode=pl.Buffered(1)),
            pl.BlockSpec((block, freq_count * LANES), lambda g: (g, 0)),
        ],
        out_specs=pl.BlockSpec((1, block), lambda g: (0, g)),
        scratch_shapes=[
            pltpu.VMEM((2, class_count, freq_count * LANES), jnp.bfloat16),
            pltpu.VMEM((class_count // 8, 8 * (last + 1), block), jnp.float32),
            pltpu.VMEM((class_count // 8, 8 * (last - 1), block), jnp.float32),
        ],
        compiler_params=pltpu.CompilerParams(vmem_limit_bytes=VMEM_LIMIT),
        cost_estimate=pl.CostEstimate(
            flops=20_000_000_000, bytes_accessed=20_000_000, transcendentals=0
        ),
        name="score",
    )(cos_mat, sin_mat, panels, spectra)
    best_score = best_score.reshape(count_p)

    first_class = lax.axis_index("cls") * classes_dev
    own_classes = first_class + jnp.arange(classes_dev, dtype=jnp.int32)
    counts = jnp.sum((all_labels[None, :] == own_classes[:, None]).astype(jnp.float32), axis=1)
    new_references = totals.astype(jnp.float32) / (counts + 1.0)[None, :, None]
    return (best_score, new_references)


def solution(mesh):
    return jax.shard_map(
        local,
        mesh=mesh,
        in_specs=(
            P(("cls", "ptl"), None, None),
            P("ptl", "cls", None),
            P(("cls", "ptl")),
            P(("cls", "ptl")),
        ),
        out_specs=(P(("cls", "ptl")), P("ptl", "cls", None)),
        check_vma=False,
    )
```

```python
import functools
import math

import jax
import jax.numpy as jnp
import numpy as np
from jax import lax
from jax.experimental import pallas as pl
from jax.experimental.pallas import tpu as pltpu
from jax.sharding import PartitionSpec as P

ROTS = 36
LANES = 128
VMEM_LIMIT = 62 * 1024 * 1024
NT = (((1,), (1,)), ((), ()))


def fold_groups(freq_count, turns):
    groups = [[] for _ in range(turns // 2 + 1)]
    for m in range(freq_count):
        rest = m % turns
        if rest <= turns // 2:
            groups[rest].append((m, 1))
        else:
            groups[turns - rest].append((m, -1))
    return groups


def spectrum_table(angles, freq_count):
    position = jnp.arange(angles, dtype=jnp.int32)
    freq_index = jnp.arange(freq_count, dtype=jnp.int32)
    phases = (
        2.0
        * math.pi
        / angles
        * (position[:, None] * freq_index[None, :] % angles).astype(jnp.float32)
    )
    factor = 1.0 / math.sqrt(angles)
    return (jnp.concatenate([jnp.cos(phases), -jnp.sin(phases)], axis=1) * factor).astype(
        jnp.bfloat16
    )


def swap_halves(panel):
    half = panel.shape[-1] // 2
    return pltpu.roll(panel, half, panel.ndim - 1)


def flip_bit(index, bit):
    step = 1 << bit
    return index + step * (1 - 2 * ((index // step) % 2))


def subsets(bits):
    out = [()]
    for bit in bits:
        out = out + [taken + (bit,) for taken in out]
    return out


def flip_bits(index, bits):
    for bit in bits:
        index = flip_bit(index, bit)
    return index


def bit_count(size):
    return size.bit_length() - 1


def main_kernel(
    groups,
    columns,
    step_pairs,
    dft_steps,
    owners,
    peers,
    rows_used,
    block,
    table_ref,
    low_ref,
    high_ref,
    class_ref,
    cos_ref,
    sin_ref,
    cos_mat_ref,
    sin_mat_ref,
    own_ref,
    best_ref,
    totals_ref,
    counts_ref,
    raw_ref,
    held_ref,
    panels_ref,
    sums_ref,
    landed_ref,
    last_ref,
    stacked_ref,
    even_ref,
    odd_ref,
    gather_z_send,
    gather_z_recv,
    gather_send,
    gather_recv,
    scatter_send,
    scatter_recv,
    scatter_z_send,
    scatter_z_recv,
):
    step = pl.program_id(0)
    freq_count = len(columns)
    half = LANES // 2
    row_count = own_ref.shape[0]
    freqs_dev = freq_count // peers
    class_rows = owners * rows_used
    last = len(groups) - 1
    bits = bit_count(peers)
    me_z = lax.axis_index("cls")
    me = lax.axis_index("ptl")
    half_rows = [slice(0, row_count // 2), slice(row_count // 2, row_count)]
    down = list(range(bits))[::-1]
    up = list(range(bits))
    gather_orders = [down, [down[1], down[0]] + down[2:]]
    scatter_orders = [up, up[:-2] + [up[-1], up[-2]]]

    def gather_z_copies():
        return [
            pltpu.make_async_remote_copy(
                src_ref=own_ref,
                dst_ref=panels_ref.at[me, me_z],
                send_sem=gather_z_send.at[d - 1],
                recv_sem=gather_z_recv.at[d - 1],
                device_id=(lax.rem(me_z + d, owners), me),
                device_id_type=pl.DeviceIdType.MESH,
            )
            for d in range(1, owners)
        ]

    def gather_copies(phase):
        out = []
        for side, order in enumerate(gather_orders):
            partner = flip_bit(me, order[phase])
            for n, taken in enumerate(subsets(order[:phase])):
                part = panels_ref.at[flip_bits(me, taken), :, half_rows[side], :]
                out.append(
                    pltpu.make_async_remote_copy(
                        src_ref=part,
                        dst_ref=part,
                        send_sem=gather_send.at[side, (1 << phase) - 1 + n],
                        recv_sem=gather_recv.at[side, (1 << phase) - 1 + n],
                        device_id=(me_z, partner),
                        device_id_type=pl.DeviceIdType.MESH,
                    )
                )
        return out

    def scatter_slots(phase):
        return subsets(range(bits - 1 - phase)), sum(1 << (bits - 1 - k) for k in range(phase))

    def scatter_copies(phase):
        out = []
        for side, order in enumerate(scatter_orders):
            partner = flip_bit(me, order[phase])
            _, base = scatter_slots(phase)
            for n, taken in enumerate(subsets(order[phase + 1 :])):
                out.append(
                    pltpu.make_async_remote_copy(
                        src_ref=sums_ref.at[flip_bits(partner, taken), :, :, half_rows[side], :],
                        dst_ref=landed_ref.at[base + n, :, :, half_rows[side], :],
                        send_sem=scatter_send.at[side, base + n],
                        recv_sem=scatter_recv.at[side, base + n],
                        device_id=(me_z, partner),
                        device_id_type=pl.DeviceIdType.MESH,
                    )
                )
        return out

    def scatter_add(phase):
        for copy in scatter_copies(phase):
            copy.wait()
        _, base = scatter_slots(phase)
        for side, order in enumerate(scatter_orders):
            rows = half_rows[side]
            for n, taken in enumerate(subsets(order[phase + 1 :])):
                kept = flip_bits(me, taken)
                sums_ref[kept, :, :, rows, :] = (
                    sums_ref[kept, :, :, rows, :].astype(jnp.float32)
                    + landed_ref[base + n, :, :, rows, :].astype(jnp.float32)
                ).astype(jnp.bfloat16)

    def scatter_z_copies():
        out = []
        for d in range(1, owners):
            target = lax.rem(me_z + d, owners)
            out.append(
                pltpu.make_async_remote_copy(
                    src_ref=sums_ref.at[me, :, target],
                    dst_ref=last_ref.at[d - 1],
                    send_sem=scatter_z_send.at[d - 1],
                    recv_sem=scatter_z_recv.at[d - 1],
                    device_id=(target, me),
                    device_id_type=pl.DeviceIdType.MESH,
                )
            )
        return out

    @pl.when(step == 0)
    def _():
        barrier = pltpu.get_barrier_semaphore()
        for d in range(1, owners):
            pl.semaphore_signal(
                barrier,
                inc=1,
                device_id=(lax.rem(me_z + d, owners), me),
                device_id_type=pl.DeviceIdType.MESH,
            )
        for bit in range(bits):
            pl.semaphore_signal(
                barrier,
                inc=1,
                device_id=(me_z, flip_bit(me, bit)),
                device_id_type=pl.DeviceIdType.MESH,
            )
        pl.semaphore_wait(barrier, owners - 1 + bits)
        panels_ref[me, me_z] = own_ref[...]
        for copy in gather_z_copies():
            copy.start()

    gather_at = [dft_steps * (k + 1) // (bits + 1) + 1 for k in range(bits - 1)] + [dft_steps]
    for phase in range(bits):

        @pl.when(step == gather_at[phase])
        def _(phase=phase):
            for copy in gather_z_copies() if phase == 0 else gather_copies(phase - 1):
                copy.wait()
            for copy in gather_copies(phase):
                copy.start()

    @pl.when(step < dft_steps)
    def _():
        table = table_ref[...]
        together = 4

        def pair_step(at, carry):
            for k in range(together):
                pair = at * together + k
                rows = jnp.concatenate([low_ref[pair], high_ref[pair]], axis=0)
                raw_ref[pl.ds(pair, 2 * freq_count, stride=step_pairs), :] = lax.dot_general(
                    table, rows, NT, preferred_element_type=jnp.float32
                )
            return carry

        lax.fori_loop(0, step_pairs // together, pair_step, 0)
        first_half = lax.broadcasted_iota(jnp.int32, (step_pairs, LANES), 1) < half
        own_rows = pl.ds(pl.multiple_of(step * step_pairs, step_pairs), step_pairs)
        for m in range(freq_count):
            real = raw_ref[m * step_pairs : (m + 1) * step_pairs, :]
            imag = raw_ref[(freq_count + m) * step_pairs : (freq_count + m + 1) * step_pairs, :]
            at = slice(columns[m] * LANES, (columns[m] + 1) * LANES)
            held_ref[0, own_rows, at] = jnp.where(first_half, real, swap_halves(imag)).astype(
                jnp.bfloat16
            )
            held_ref[1, own_rows, at] = jnp.where(first_half, swap_halves(real), imag).astype(
                jnp.bfloat16
            )

    @pl.when(step == dft_steps)
    def _():
        count_p = class_ref.shape[1]
        half_p = count_p // 2
        member = lax.broadcasted_iota(jnp.int32, (class_rows, count_p), 0) == class_ref[...]
        lane = lax.broadcasted_iota(jnp.int32, (class_rows, LANES), 1)
        flip = jnp.where(lane < half, 1.0, -1.0)
        padding = jnp.zeros((row_count - rows_used, LANES), jnp.float32)
        column = 0
        for folded, group in enumerate(groups):
            at = slice(column, column + len(group) * LANES)
            column += len(group) * LANES
            weights = jnp.concatenate(
                [
                    jnp.where(member, cos_ref[folded : folded + 1, :], 0.0),
                    jnp.where(member, sin_ref[folded : folded + 1, :], 0.0),
                ],
                axis=0,
            ).astype(jnp.bfloat16)
            both = jnp.dot(
                weights[:, :half_p], held_ref[0, :, at], preferred_element_type=jnp.float32
            ) + jnp.dot(
                weights[:, half_p:], held_ref[1, :, at], preferred_element_type=jnp.float32
            )
            for place, (m, sign) in enumerate(group):
                part = both[:, place * LANES : (place + 1) * LANES]
                turned = swap_halves(part[class_rows:]) * flip
                total = part[:class_rows] + (turned if sign > 0 else -turned)
                for owner in range(owners):
                    sums_ref[m // freqs_dev, m % freqs_dev, owner] = jnp.concatenate(
                        [total[owner * rows_used : (owner + 1) * rows_used], padding], axis=0
                    ).astype(jnp.bfloat16)
        for copy in scatter_copies(0):
            copy.start()

    @pl.when(step == dft_steps + 1)
    def _():
        for copy in gather_copies(bits - 1):
            copy.wait()
        lane = lax.broadcasted_iota(jnp.int32, (rows_used, LANES), 1)
        flip = jnp.where(lane < half, 1.0, -1.0)
        for m in range(freq_count):
            sign = [s for group in groups for k, s in group if k == m][0]
            weight = 1.0 if m == 0 else 2.0
            at = slice(columns[m] * LANES, (columns[m] + 1) * LANES)
            source = slice(m % freqs_dev * LANES, (m % freqs_dev + 1) * LANES)
            for owner in range(owners):
                panel = panels_ref[m // freqs_dev, owner, :rows_used, source]
                panel = panel.astype(jnp.float32) * weight
                rows = slice(owner * rows_used, (owner + 1) * rows_used)
                stacked_ref[0, rows, at] = panel.astype(jnp.bfloat16)
                stacked_ref[1, rows, at] = (swap_halves(panel) * (flip * sign)).astype(
                    jnp.bfloat16
                )
        counts = jnp.zeros((row_count, LANES), jnp.float32)
        for peer in range(peers):
            for owner in range(owners):
                counts += panels_ref[peer, owner, :, freqs_dev * LANES :].astype(jnp.float32)
        counts_ref[...] = counts
        scatter_add(0)
        for copy in scatter_copies(1):
            copy.start()

    @pl.when(step >= dft_steps + 2)
    def _():
        tiles = class_rows // 8
        chunk = step - (dft_steps + 2)
        row = chunk * block
        half_p = held_ref.shape[1]
        rows = pl.ds(pl.multiple_of(row % half_p, block), block)
        column = 0
        for folded, group in enumerate(groups):
            at = slice(column, column + len(group) * LANES)
            column += len(group) * LANES
            taken = held_ref[row // half_p, rows, at]
            even = lax.dot_general(
                stacked_ref[0, :, at], taken, NT, preferred_element_type=jnp.float32
            )
            even_ref[:, folded * 8 : (folded + 1) * 8, :] = even.reshape(tiles, 8, -1)
            if 0 < folded < last:
                odd = lax.dot_general(
                    stacked_ref[1, :, at], taken, NT, preferred_element_type=jnp.float32
                )
                odd_ref[:, (folded - 1) * 8 : folded * 8, :] = odd.reshape(tiles, 8, -1)

        for phase in range(1, bits):

            @pl.when(chunk == min(phase - 1, 1))
            def _(phase=phase):
                scatter_add(phase)
                for copy in scatter_copies(phase + 1) if phase + 1 < bits else scatter_z_copies():
                    copy.start()

        cos_mat, sin_mat = cos_mat_ref[...], sin_mat_ref[...]

        def tile_step(tile, best):
            even = jnp.dot(
                cos_mat, even_ref[tile].astype(jnp.bfloat16), preferred_element_type=jnp.float32
            )
            odd = jnp.dot(
                sin_mat, odd_ref[tile].astype(jnp.bfloat16), preferred_element_type=jnp.float32
            )
            best = jnp.maximum(best, jnp.maximum(even[:8], even[last * 8 :]))
            for turn in range(1, last):
                best = jnp.maximum(
                    best,
                    even[turn * 8 : (turn + 1) * 8] + jnp.abs(odd[(turn - 1) * 8 : turn * 8]),
                )
            return best

        best = lax.fori_loop(0, tiles, tile_step, jnp.full((8, block), -jnp.inf, jnp.float32))
        best_ref[0] = jnp.max(best, axis=0, keepdims=True)

        @pl.when(step == pl.num_programs(0) - 1)
        def _():
            for copy in scatter_z_copies():
                copy.wait()
            total = sums_ref[me, :, me_z].astype(jnp.float32)
            for d in range(1, owners):
                total += last_ref[d - 1].astype(jnp.float32)
            totals_ref[...] = total


def local(particles, references, best_class, best_turn):
    count_p, cycle_count, angles = particles.shape
    freq_count = angles // 2
    groups = fold_groups(freq_count, ROTS)
    last = len(groups) - 1
    columns = [0] * freq_count
    place = 0
    for group in groups:
        for m, _ in group:
            columns[m] = place
            place += 1
    owners, peers = lax.axis_size("cls"), lax.axis_size("ptl")
    bits = bit_count(peers)
    freqs_dev, classes_dev, _ = references.shape
    rows_used = -(-classes_dev // 8) * 8
    row_count = -(-classes_dev // 32) * 32
    class_rows = owners * rows_used

    own = jnp.transpose(references, (1, 0, 2)).reshape(classes_dev, freqs_dev * LANES)
    own = jnp.concatenate([own, own[: row_count - classes_dev]], axis=0)
    owner_of = best_class // classes_dev
    local_class = best_class - owner_of * classes_dev
    row_of = jnp.where(
        jnp.arange(LANES, dtype=jnp.int32)[None, :] == owner_of[:, None], local_class[:, None], -1
    )
    own_counts = jnp.sum(
        (
            row_of[:, None, :owners] == jnp.arange(row_count, dtype=jnp.int32)[None, :, None]
        ).astype(jnp.float32),
        axis=0,
    )
    own_counts = jnp.pad(own_counts, ((0, 0), (0, LANES - owners)))
    own = jnp.concatenate([own, own_counts.astype(jnp.bfloat16)], axis=1)

    step_pairs = 32
    pairs = count_p // 2
    dft_steps = pairs // step_pairs
    folded_index = jnp.arange(last + 1, dtype=jnp.int32)
    phases = (
        2.0
        * math.pi
        / ROTS
        * (folded_index[:, None] * best_turn[None, :] % ROTS).astype(jnp.float32)
    )
    table = spectrum_table(angles, freq_count).T
    turn_index = np.arange(last + 1)
    turn_phase = 2.0 * math.pi / ROTS * (turn_index[:, None] * turn_index[None, :] % ROTS)
    spread = np.eye(8, dtype=np.float32)
    cos_mat = jnp.asarray(np.kron(np.cos(turn_phase).astype(np.float32), spread), jnp.bfloat16)
    sin_mat = jnp.asarray(
        np.kron(-np.sin(turn_phase[1:last, 1:last]).astype(np.float32), spread), jnp.bfloat16
    )
    block = min(256 if class_rows <= 256 else 128, pairs)
    chunks = count_p // block
    whole = lambda *_: (0, 0)
    best_score, totals, counts = pl.pallas_call(
        functools.partial(
            main_kernel,
            groups,
            columns,
            step_pairs,
            dft_steps,
            owners,
            peers,
            rows_used,
            block,
        ),
        grid=(dft_steps + 2 + chunks,),
        out_shape=(
            jax.ShapeDtypeStruct((chunks, 1, block), jnp.float32),
            jax.ShapeDtypeStruct((freqs_dev, row_count, LANES), jnp.float32),
            jax.ShapeDtypeStruct((row_count, LANES), jnp.float32),
        ),
        in_specs=[
            pl.BlockSpec((angles, 2 * freq_count), whole),
            pl.BlockSpec(
                (step_pairs, cycle_count, angles),
                lambda g: (jnp.minimum(g, dft_steps - 1), 0, 0),
            ),
            pl.BlockSpec(
                (step_pairs, cycle_count, angles),
                lambda g: (jnp.minimum(g, dft_steps - 1) + dft_steps, 0, 0),
            ),
            pl.BlockSpec((1, count_p), whole),
            pl.BlockSpec((last + 1, count_p), whole),
            pl.BlockSpec((last + 1, count_p), whole),
            pl.BlockSpec(cos_mat.shape, whole),
            pl.BlockSpec(sin_mat.shape, whole),
            pl.BlockSpec(memory_space=pltpu.VMEM),
        ],
        out_specs=(
            pl.BlockSpec((1, 1, block), lambda g: (jnp.maximum(g - dft_steps - 2, 0), 0, 0)),
            pl.BlockSpec(memory_space=pltpu.VMEM),
            pl.BlockSpec(memory_space=pltpu.VMEM),
        ),
        scratch_shapes=[
            pltpu.VMEM((2 * freq_count * step_pairs, LANES), jnp.float32),
            pltpu.VMEM((2, pairs, freq_count * LANES), jnp.bfloat16),
            pltpu.VMEM((peers, owners, row_count, (freqs_dev + 1) * LANES), jnp.bfloat16),
            pltpu.VMEM((peers, freqs_dev, owners, row_count, LANES), jnp.bfloat16),
            pltpu.VMEM((peers - 1, freqs_dev, owners, row_count, LANES), jnp.bfloat16),
            pltpu.VMEM((owners - 1, freqs_dev, row_count, LANES), jnp.bfloat16),
            pltpu.VMEM((2, class_rows, freq_count * LANES), jnp.bfloat16),
            pltpu.VMEM((class_rows // 8, 8 * (last + 1), block), jnp.float32),
            pltpu.VMEM((class_rows // 8, 8 * (last - 1), block), jnp.float32),
            pltpu.SemaphoreType.DMA((owners - 1,)),
            pltpu.SemaphoreType.DMA((owners - 1,)),
            pltpu.SemaphoreType.DMA((2, peers - 1)),
            pltpu.SemaphoreType.DMA((2, peers - 1)),
            pltpu.SemaphoreType.DMA((2, peers - 1)),
            pltpu.SemaphoreType.DMA((2, peers - 1)),
            pltpu.SemaphoreType.DMA((owners - 1,)),
            pltpu.SemaphoreType.DMA((owners - 1,)),
        ],
        compiler_params=pltpu.CompilerParams(
            vmem_limit_bytes=VMEM_LIMIT, collective_id=0, has_side_effects=True
        ),
        name="classify",
    )(
        table,
        particles,
        particles,
        (owner_of * rows_used + local_class).reshape(1, count_p),
        jnp.cos(phases),
        jnp.sin(phases),
        cos_mat,
        sin_mat,
        own,
    )
    my_counts = lax.dynamic_slice_in_dim(counts, lax.axis_index("cls"), 1, axis=1)
    new_references = totals[:, :classes_dev] / (my_counts[None, :classes_dev] + 1.0)
    return (best_score.reshape(count_p), new_references)


def solution(mesh):
    return jax.shard_map(
        local,
        mesh=mesh,
        in_specs=(
            P(("cls", "ptl"), None, None),
            P("ptl", "cls", None),
            P(("cls", "ptl")),
            P(("cls", "ptl")),
        ),
        out_specs=(P(("cls", "ptl")), P("ptl", "cls", None)),
        check_vma=False,
    )
```

```python
import functools
import math

import jax
import jax.numpy as jnp
import numpy as np
from jax import lax
from jax.experimental import pallas as pl
from jax.experimental.pallas import tpu as pltpu
from jax.sharding import PartitionSpec as P

ROTS = 36
LANES = 128
VMEM_LIMIT = 62 * 1024 * 1024
NT = (((1,), (1,)), ((), ()))


def fold_groups(freq_count, turns):
    groups = [[] for _ in range(turns // 2 + 1)]
    for m in range(freq_count):
        rest = m % turns
        if rest <= turns // 2:
            groups[rest].append((m, 1))
        else:
            groups[turns - rest].append((m, -1))
    return groups


def swap_halves(panel):
    half = panel.shape[-1] // 2
    return pltpu.roll(panel, half, panel.ndim - 1)


def flip_bit(index, bit):
    step = 1 << bit
    return index + step * (1 - 2 * ((index // step) % 2))


def subsets(bits):
    out = [()]
    for bit in bits:
        out = out + [taken + (bit,) for taken in out]
    return out


def flip_bits(index, bits):
    for bit in bits:
        index = flip_bit(index, bit)
    return index


def bit_count(size):
    return size.bit_length() - 1


def main_kernel(
    groups,
    columns,
    step_pairs,
    dft_steps,
    owners,
    peers,
    rows_used,
    block,
    table_ref,
    low_ref,
    high_ref,
    class_ref,
    turn_ref,
    turn_table_ref,
    cos_mat_ref,
    sin_mat_ref,
    own_ref,
    best_ref,
    totals_ref,
    counts_ref,
    raw_ref,
    held_ref,
    panels_ref,
    sums_ref,
    landed_ref,
    last_ref,
    stacked_ref,
    even_ref,
    odd_ref,
    gather_z_send,
    gather_z_recv,
    gather_send,
    gather_recv,
    scatter_send,
    scatter_recv,
    scatter_z_send,
    scatter_z_recv,
):
    step = pl.program_id(0)
    freq_count = len(columns)
    half = LANES // 2
    freqs_dev = freq_count // peers
    own_rows, sum_rows = own_ref.shape[0], freqs_dev * rows_used
    class_rows = owners * rows_used
    last = len(groups) - 1
    bits = bit_count(peers)
    me_z = lax.axis_index("cls")
    me = lax.axis_index("ptl")
    gather_rows = [slice(0, own_rows // 2), slice(own_rows // 2, own_rows)]
    half_rows = [slice(0, sum_rows // 2), slice(sum_rows // 2, sum_rows)]
    down = list(range(bits))[::-1]
    up = list(range(bits))
    gather_orders = [down, [down[1], down[0]] + down[2:]]
    scatter_orders = [up, up[:-2] + [up[-1], up[-2]]]

    def gather_z_copies():
        return [
            pltpu.make_async_remote_copy(
                src_ref=own_ref,
                dst_ref=panels_ref.at[me, me_z],
                send_sem=gather_z_send.at[d - 1],
                recv_sem=gather_z_recv.at[d - 1],
                device_id=(lax.rem(me_z + d, owners), me),
                device_id_type=pl.DeviceIdType.MESH,
            )
            for d in range(1, owners)
        ]

    def gather_copies(phase):
        out = []
        for side, order in enumerate(gather_orders):
            partner = flip_bit(me, order[phase])
            for n, taken in enumerate(subsets(order[:phase])):
                part = panels_ref.at[flip_bits(me, taken), :, gather_rows[side], :]
                out.append(
                    pltpu.make_async_remote_copy(
                        src_ref=part,
                        dst_ref=part,
                        send_sem=gather_send.at[side, (1 << phase) - 1 + n],
                        recv_sem=gather_recv.at[side, (1 << phase) - 1 + n],
                        device_id=(me_z, partner),
                        device_id_type=pl.DeviceIdType.MESH,
                    )
                )
        return out

    def scatter_slots(phase):
        return subsets(range(bits - 1 - phase)), sum(1 << (bits - 1 - k) for k in range(phase))

    def scatter_copies(phase):
        out = []
        for side, order in enumerate(scatter_orders):
            partner = flip_bit(me, order[phase])
            _, base = scatter_slots(phase)
            for n, taken in enumerate(subsets(order[phase + 1 :])):
                out.append(
                    pltpu.make_async_remote_copy(
                        src_ref=sums_ref.at[flip_bits(partner, taken), :, half_rows[side], :],
                        dst_ref=landed_ref.at[base + n, :, half_rows[side], :],
                        send_sem=scatter_send.at[side, base + n],
                        recv_sem=scatter_recv.at[side, base + n],
                        device_id=(me_z, partner),
                        device_id_type=pl.DeviceIdType.MESH,
                    )
                )
        return out

    def scatter_add(phase):
        for copy in scatter_copies(phase):
            copy.wait()
        _, base = scatter_slots(phase)
        for side, order in enumerate(scatter_orders):
            rows = half_rows[side]
            for n, taken in enumerate(subsets(order[phase + 1 :])):
                kept = flip_bits(me, taken)
                sums_ref[kept, :, rows, :] = (
                    sums_ref[kept, :, rows, :].astype(jnp.float32)
                    + landed_ref[base + n, :, rows, :].astype(jnp.float32)
                ).astype(jnp.bfloat16)

    def scatter_z_copies():
        out = []
        for d in range(1, owners):
            target = lax.rem(me_z + d, owners)
            out.append(
                pltpu.make_async_remote_copy(
                    src_ref=sums_ref.at[me, target],
                    dst_ref=last_ref.at[d - 1],
                    send_sem=scatter_z_send.at[d - 1],
                    recv_sem=scatter_z_recv.at[d - 1],
                    device_id=(target, me),
                    device_id_type=pl.DeviceIdType.MESH,
                )
            )
        return out

    @pl.when(step == 0)
    def _():
        barrier = pltpu.get_barrier_semaphore()
        for d in range(1, owners):
            pl.semaphore_signal(
                barrier,
                inc=1,
                device_id=(lax.rem(me_z + d, owners), me),
                device_id_type=pl.DeviceIdType.MESH,
            )
        for bit in range(bits):
            pl.semaphore_signal(
                barrier,
                inc=1,
                device_id=(me_z, flip_bit(me, bit)),
                device_id_type=pl.DeviceIdType.MESH,
            )
        pl.semaphore_wait(barrier, owners - 1 + bits)
        panels_ref[me, me_z] = own_ref[...]
        for copy in gather_z_copies():
            copy.start()

    gather_at = [dft_steps * (k + 1) // bits + 1 for k in range(bits - 1)] + [dft_steps + 1]
    for phase in range(bits):

        @pl.when(step == gather_at[phase])
        def _(phase=phase):
            for copy in gather_z_copies() if phase == 0 else gather_copies(phase - 1):
                copy.wait()
            for copy in gather_copies(phase):
                copy.start()

    @pl.when(step < dft_steps)
    def _():
        table = table_ref[...]
        for start in range(0, step_pairs, 8):
            rows = jnp.concatenate(
                [ref[start + k] for k in range(8) for ref in (low_ref, high_ref)], axis=0
            )
            raw = lax.dot_general(table, rows, NT, preferred_element_type=jnp.float32)
            raw = jnp.stack([raw[:, k * LANES : (k + 1) * LANES] for k in range(8)], axis=0)
            raw_ref[:, start : start + 8, :] = jnp.swapaxes(raw, 0, 1)
        first_half = lax.broadcasted_iota(jnp.int32, (step_pairs, LANES), 1) < half
        own_rows = pl.ds(pl.multiple_of(step * step_pairs, step_pairs), step_pairs)
        for m in range(freq_count):
            real = raw_ref[m]
            imag = raw_ref[freq_count + m]
            at = slice(columns[m] * LANES, (columns[m] + 1) * LANES)
            held_ref[0, own_rows, at] = jnp.where(first_half, real, swap_halves(imag)).astype(
                jnp.bfloat16
            )
            held_ref[1, own_rows, at] = jnp.where(first_half, swap_halves(real), imag).astype(
                jnp.bfloat16
            )

    @pl.when(step == dft_steps)
    def _():
        count_p = class_ref.shape[1]
        half_p = count_p // 2
        member = lax.broadcasted_iota(jnp.int32, (class_rows, count_p), 0) == class_ref[...]
        turns = turn_table_ref.shape[2]
        at_turn = lax.broadcasted_iota(jnp.int32, (turns, count_p), 0) == turn_ref[...]
        at_turn = jnp.where(at_turn, 1.0, 0.0).astype(jnp.bfloat16)
        cosines = jnp.dot(turn_table_ref[0], at_turn, preferred_element_type=jnp.float32)
        sines = jnp.dot(turn_table_ref[1], at_turn, preferred_element_type=jnp.float32)
        lane = lax.broadcasted_iota(jnp.int32, (class_rows, LANES), 1)
        flip = jnp.where(lane < half, 1.0, -1.0)
        column = 0
        for folded, group in enumerate(groups):
            at = slice(column, column + len(group) * LANES)
            column += len(group) * LANES
            weights = jnp.concatenate(
                [
                    jnp.where(member, cosines[folded : folded + 1, :], 0.0),
                    jnp.where(member, sines[folded : folded + 1, :], 0.0),
                ],
                axis=0,
            ).astype(jnp.bfloat16)
            both = jnp.dot(
                weights[:, :half_p], held_ref[0, :, at], preferred_element_type=jnp.float32
            ) + jnp.dot(
                weights[:, half_p:], held_ref[1, :, at], preferred_element_type=jnp.float32
            )
            for place, (m, sign) in enumerate(group):
                part = both[:, place * LANES : (place + 1) * LANES]
                turned = swap_halves(part[class_rows:]) * flip
                total = part[:class_rows] + (turned if sign > 0 else -turned)
                for owner in range(owners):
                    row = m % freqs_dev * rows_used
                    sums_ref[m // freqs_dev, owner, row : row + rows_used, :] = total[
                        owner * rows_used : (owner + 1) * rows_used
                    ].astype(jnp.bfloat16)
        for copy in scatter_copies(0):
            copy.start()

    @pl.when(step == dft_steps + 1)
    def _():
        scatter_add(0)
        for copy in scatter_copies(1):
            copy.start()
        for copy in gather_copies(bits - 1):
            copy.wait()
        lane = lax.broadcasted_iota(jnp.int32, (rows_used, LANES), 1)
        flip = jnp.where(lane < half, 1.0, -1.0)
        for m in range(freq_count):
            sign = [s for group in groups for k, s in group if k == m][0]
            weight = 1.0 if m == 0 else 2.0
            at = slice(columns[m] * LANES, (columns[m] + 1) * LANES)
            source = slice(m % freqs_dev * rows_used, (m % freqs_dev + 1) * rows_used)
            for owner in range(owners):
                panel = panels_ref[m // freqs_dev, owner, source, :]
                panel = panel.astype(jnp.float32) * weight
                rows = slice(owner * rows_used, (owner + 1) * rows_used)
                stacked_ref[0, rows, at] = panel.astype(jnp.bfloat16)
                stacked_ref[1, rows, at] = (swap_halves(panel) * (flip * sign)).astype(
                    jnp.bfloat16
                )
        counts = jnp.zeros(counts_ref.shape, jnp.float32)
        for peer in range(peers):
            for owner in range(owners):
                counts += panels_ref[peer, owner, sum_rows:, :].astype(jnp.float32)
        counts_ref[...] = counts

    @pl.when(step >= dft_steps + 2)
    def _():
        tiles = class_rows // 8
        chunk = step - (dft_steps + 2)
        row = chunk * block
        half_p = held_ref.shape[1]
        rows = pl.ds(pl.multiple_of(row % half_p, block), block)

        def reduce_further(at_chunk, phases):
            @pl.when(chunk == at_chunk)
            def _():
                for phase in phases:
                    scatter_add(phase)
                    more = scatter_copies(phase + 1) if phase + 1 < bits else scatter_z_copies()
                    for copy in more:
                        copy.start()

        column = 0
        for folded, group in enumerate(groups):
            if folded == len(groups) // 3:
                reduce_further(1, range(2, bits))
            at = slice(column, column + len(group) * LANES)
            column += len(group) * LANES
            taken = held_ref[row // half_p, rows, at]
            even = lax.dot_general(
                stacked_ref[0, :, at], taken, NT, preferred_element_type=jnp.float32
            )
            even_ref[:, folded * 8 : (folded + 1) * 8, :] = even.reshape(tiles, 8, -1)
            if 0 < folded < last:
                odd = lax.dot_general(
                    stacked_ref[1, :, at], taken, NT, preferred_element_type=jnp.float32
                )
                odd_ref[:, (folded - 1) * 8 : folded * 8, :] = odd.reshape(tiles, 8, -1)

        reduce_further(0, range(1, 2))
        cos_mat, sin_mat = cos_mat_ref[...], sin_mat_ref[...]

        def tile_step(tile, best):
            even = jnp.dot(
                cos_mat, even_ref[tile].astype(jnp.bfloat16), preferred_element_type=jnp.float32
            )
            odd = jnp.dot(
                sin_mat, odd_ref[tile].astype(jnp.bfloat16), preferred_element_type=jnp.float32
            )
            best = jnp.maximum(best, jnp.maximum(even[:8], even[last * 8 :]))
            for turn in range(1, last):
                best = jnp.maximum(
                    best,
                    even[turn * 8 : (turn + 1) * 8] + jnp.abs(odd[(turn - 1) * 8 : turn * 8]),
                )
            return best

        best = lax.fori_loop(0, tiles, tile_step, jnp.full((8, block), -jnp.inf, jnp.float32))
        best_ref[0] = jnp.max(best, axis=0, keepdims=True)

        @pl.when(step == pl.num_programs(0) - 1)
        def _():
            for copy in scatter_z_copies():
                copy.wait()
            total = sums_ref[me, me_z].astype(jnp.float32)
            for d in range(1, owners):
                total += last_ref[d - 1].astype(jnp.float32)
            totals_ref[...] = total


def local(particles, references, best_class, best_turn):
    count_p, cycle_count, angles = particles.shape
    freq_count = angles // 2
    groups = fold_groups(freq_count, ROTS)
    last = len(groups) - 1
    columns = [0] * freq_count
    place = 0
    for group in groups:
        for m, _ in group:
            columns[m] = place
            place += 1
    owners, peers = lax.axis_size("cls"), lax.axis_size("ptl")
    bits = bit_count(peers)
    freqs_dev, classes_dev, _ = references.shape
    rows_used = -(-classes_dev // 8) * 8
    sum_rows = freqs_dev * rows_used
    row_count = -(-(sum_rows + classes_dev) // 32) * 32 - sum_rows
    class_rows = owners * rows_used

    owner_of = best_class // classes_dev
    local_class = best_class - owner_of * classes_dev
    row_of = jnp.where(
        jnp.arange(LANES, dtype=jnp.int32)[None, :] == owner_of[:, None], local_class[:, None], -1
    )
    own_counts = jnp.sum(
        (
            row_of[:, None, :owners] == jnp.arange(row_count, dtype=jnp.int32)[None, :, None]
        ).astype(jnp.float32),
        axis=0,
    )
    own_counts = jnp.pad(own_counts, ((0, 0), (0, LANES - owners)))
    padded = jnp.concatenate([references, references[:, : rows_used - classes_dev]], axis=1)
    own = jnp.concatenate(
        [padded.reshape(freqs_dev * rows_used, LANES), own_counts.astype(jnp.bfloat16)], axis=0
    )

    step_pairs = 32
    pairs = count_p // 2
    dft_steps = pairs // step_pairs
    angle = 2.0 * math.pi / angles * (np.outer(np.arange(freq_count), np.arange(angles)) % angles)
    table = np.concatenate([np.cos(angle), -np.sin(angle)], axis=0) / math.sqrt(angles)
    table = jnp.asarray(table.astype(np.float32), jnp.bfloat16)
    turn = 2.0 * math.pi / ROTS * (np.outer(np.arange(last + 1), np.arange(ROTS)) % ROTS)
    turn_table = np.zeros((2, -(-(last + 1) // 16) * 16, -(-ROTS // 16) * 16), np.float32)
    turn_table[0, : last + 1, :ROTS] = np.cos(turn)
    turn_table[1, : last + 1, :ROTS] = np.sin(turn)
    turn_table = jnp.asarray(turn_table, jnp.bfloat16)
    turn_index = np.arange(last + 1)
    turn_phase = 2.0 * math.pi / ROTS * (turn_index[:, None] * turn_index[None, :] % ROTS)
    spread = np.eye(8, dtype=np.float32)
    cos_mat = jnp.asarray(np.kron(np.cos(turn_phase).astype(np.float32), spread), jnp.bfloat16)
    sin_mat = jnp.asarray(
        np.kron(-np.sin(turn_phase[1:last, 1:last]).astype(np.float32), spread), jnp.bfloat16
    )
    block = min(256 if class_rows <= 256 else 128, pairs)
    chunks = count_p // block
    whole = lambda *_: (0, 0)
    best_score, totals, counts = pl.pallas_call(
        functools.partial(
            main_kernel,
            groups,
            columns,
            step_pairs,
            dft_steps,
            owners,
            peers,
            rows_used,
            block,
        ),
        grid=(dft_steps + 2 + chunks,),
        out_shape=(
            jax.ShapeDtypeStruct((chunks, 1, block), jnp.float32),
            jax.ShapeDtypeStruct((sum_rows, LANES), jnp.float32),
            jax.ShapeDtypeStruct((row_count, LANES), jnp.float32),
        ),
        in_specs=[
            pl.BlockSpec((angles, 2 * freq_count), whole),
            pl.BlockSpec(
                (step_pairs, cycle_count, angles),
                lambda g: (jnp.minimum(g, dft_steps - 1), 0, 0),
            ),
            pl.BlockSpec(
                (step_pairs, cycle_count, angles),
                lambda g: (jnp.minimum(g, dft_steps - 1) + dft_steps, 0, 0),
            ),
            pl.BlockSpec((1, count_p), whole),
            pl.BlockSpec((1, count_p), whole),
            pl.BlockSpec(turn_table.shape, lambda g: (0, 0, 0)),
            pl.BlockSpec(cos_mat.shape, whole),
            pl.BlockSpec(sin_mat.shape, whole),
            pl.BlockSpec(memory_space=pltpu.VMEM),
        ],
        out_specs=(
            pl.BlockSpec((1, 1, block), lambda g: (jnp.maximum(g - dft_steps - 2, 0), 0, 0)),
            pl.BlockSpec(memory_space=pltpu.VMEM),
            pl.BlockSpec(memory_space=pltpu.VMEM),
        ),
        scratch_shapes=[
            pltpu.VMEM((2 * freq_count, step_pairs, LANES), jnp.float32),
            pltpu.VMEM((2, pairs, freq_count * LANES), jnp.bfloat16),
            pltpu.VMEM((peers, owners, sum_rows + row_count, LANES), jnp.bfloat16),
            pltpu.VMEM((peers, owners, sum_rows, LANES), jnp.bfloat16),
            pltpu.VMEM((peers - 1, owners, sum_rows, LANES), jnp.bfloat16),
            pltpu.VMEM((owners - 1, sum_rows, LANES), jnp.bfloat16),
            pltpu.VMEM((2, class_rows, freq_count * LANES), jnp.bfloat16),
            pltpu.VMEM((class_rows // 8, 8 * (last + 1), block), jnp.float32),
            pltpu.VMEM((class_rows // 8, 8 * (last - 1), block), jnp.float32),
            pltpu.SemaphoreType.DMA((owners - 1,)),
            pltpu.SemaphoreType.DMA((owners - 1,)),
            pltpu.SemaphoreType.DMA((2, peers - 1)),
            pltpu.SemaphoreType.DMA((2, peers - 1)),
            pltpu.SemaphoreType.DMA((2, peers - 1)),
            pltpu.SemaphoreType.DMA((2, peers - 1)),
            pltpu.SemaphoreType.DMA((owners - 1,)),
            pltpu.SemaphoreType.DMA((owners - 1,)),
        ],
        compiler_params=pltpu.CompilerParams(
            vmem_limit_bytes=VMEM_LIMIT, collective_id=0, has_side_effects=True
        ),
        name="classify",
    )(
        table,
        particles,
        particles,
        (owner_of * rows_used + local_class).reshape(1, count_p),
        best_turn.reshape(1, count_p),
        turn_table,
        cos_mat,
        sin_mat,
        own,
    )
    my_counts = lax.dynamic_slice_in_dim(counts, lax.axis_index("cls"), 1, axis=1)
    totals = totals.reshape(freqs_dev, rows_used, LANES)
    new_references = totals[:, :classes_dev] / (my_counts[None, :classes_dev] + 1.0)
    return (best_score.reshape(count_p), new_references)


def solution(mesh):
    return jax.shard_map(
        local,
        mesh=mesh,
        in_specs=(
            P(("cls", "ptl"), None, None),
            P("ptl", "cls", None),
            P(("cls", "ptl")),
            P(("cls", "ptl")),
        ),
        out_specs=(P(("cls", "ptl")), P("ptl", "cls", None)),
        check_vma=False,
    )
```
